32 devices in a mesh: axial: 8 (over z, y), sector: 4 (over x, core).
Axes of the slice: x: 2, y: 2, z: 4, core: 2. Of those that a mesh axis runs over, the one named last changes fastest.
Arguments:
- start_field: float32 [5, 128, 32, 128], P(None, 'axial', 'sector'), may hold values from -6 to 6
- rhs: float32 [5, 128, 32, 128], P(None, 'axial', 'sector')
- dinv: float32 [5, 5, 128, 32, 128], P(None, None, 'axial', 'sector')
- lower: float32 [5, 5, 128, 32, 128], P(None, None, 'axial', 'sector')
- upper: float32 [5, 5, 128, 32, 128], P(None, None, 'axial', 'sector')
- az_left: float32 [5, 128, 32, 128], P(None, 'axial', 'sector')
- az_right: float32 [5, 128, 32, 128], P(None, 'axial', 'sector')
- counts: int32 [8, 4, 4], P('axial', 'sector'), may hold values from 32 to 128, as said below
- receiver_cells: int32 [8, 4, 4, 128], P('axial', 'sector'), may hold values from 0 to 16383
- donor_cell: int32 [8, 4, 4, 128], P('axial', 'sector'), may hold values from 0 to 16383
- iface_weight: float32 [8, 4, 5, 4, 128], P('axial', 'sector'), may hold values from -0.25 to 0.25
Outputs:
- adjoint_field: float32 [5, 128, 32, 128], P(None, 'axial', 'sector')
The draws below stay inside these ranges and needn't reach their ends.
Inputs may be any that keep to these rules, and one draw needn't show every extreme that they name: Only the first counts[a, s, t] slots of each (a, s, t) are live; in every segment some sector receives 128 live slots from every sector.
All inputs are finite; a program needn't handle non-finite values.
Results may differ from the reference program's by a relative error of at most 0.0001.
Values sent between devices are 32-bit elements; how exact they have to be, the bound alone decides.
A program may use at most 128 MiB of HBM per device.

```python
import math
import jax
import jax.numpy as jnp
from jax import lax

FIELDS = 5
PLANES = 16
AZ = 8
RAD = 128
CAP = 128
SWEEPS = 2
SEGS = 8
SECTORS = 4
TUBE_SLICES = 128
AZALL = 32


def log_range(key, multiway_dimension_sizes, low_end, high_end):
    return jnp.exp(jax.random.uniform(key, multiway_dimension_sizes, jnp.float32, math.log(low_end), math.log(high_end)))


def cell_law(key):
    multiway_dimension_sizes = (FIELDS, TUBE_SLICES, AZALL, RAD)
    diagonal = log_range(jax.random.fold_in(key, 11), multiway_dimension_sizes, 0.5, 2.0)
    off_diagonal = (1.0 - jnp.eye(FIELDS, dtype=jnp.float32))[:, :, None, None, None]
    mixing = 0.1 * jnp.sqrt(diagonal[:, None] * diagonal[None]) * jax.random.truncated_normal(jax.random.fold_in(key, 12), -3.0, 3.0, (FIELDS,) + multiway_dimension_sizes, jnp.float32)
    mixing = mixing * off_diagonal
    slow_share = 0.5
    slow_mask = jax.random.bernoulli(jax.random.fold_in(key, 13), slow_share, (FIELDS, 1, AZALL, RAD))
    line_shape = (FIELDS, SEGS, AZALL, RAD)
    slow_loss = log_range(jax.random.fold_in(key, 14), line_shape, 0.3, 1.0) / TUBE_SLICES
    fast_loss = log_range(jax.random.fold_in(key, 15), line_shape, 0.02, 0.05)
    base_loss = jnp.repeat(jnp.where(slow_mask, slow_loss, fast_loss), PLANES, axis=1)
    loss_rate = base_loss * log_range(jax.random.fold_in(key, 16), multiway_dimension_sizes, 0.7, 1.4)
    spike_occurrences = jax.random.randint(jax.random.fold_in(key, 17), (3,), 0, TUBE_SLICES)
    sudden_jump_indicator = jnp.any(jnp.arange(TUBE_SLICES)[:, None] == spike_occurrences[None], axis=1)[None, :, None, None]
    persistence_chance = 1.0 - loss_rate
    persisting_jumps = persistence_chance * jax.random.uniform(jax.random.fold_in(key, 18), multiway_dimension_sizes, jnp.float32, 0.5, 0.8)
    persistence_chance = jnp.where(sudden_jump_indicator, persisting_jumps, persistence_chance)
    loss_rate = 1.0 - persistence_chance
    back_rate = 0.05 * jax.random.uniform(jax.random.fold_in(key, 19), multiway_dimension_sizes, jnp.float32, 0.5, 1.5)
    left_rate = 0.15 * loss_rate * jax.random.uniform(jax.random.fold_in(key, 20), multiway_dimension_sizes, jnp.float32, 0.5, 1.5)
    right_rate = 0.15 * loss_rate * jax.random.uniform(jax.random.fold_in(key, 21), multiway_dimension_sizes, jnp.float32, 0.5, 1.5)
    downward = jax.random.bernoulli(jax.random.fold_in(key, 22), 0.5, (FIELDS, 1, AZALL, RAD))
    down_share = downward.astype(jnp.float32)
    rate_low = jnp.where(downward, persistence_chance, back_rate)
    rate_up = jnp.where(downward, back_rate, persistence_chance)
    leak_low = 0.2 * jax.random.truncated_normal(jax.random.fold_in(key, 23), -3.0, 3.0, (FIELDS,) + multiway_dimension_sizes, jnp.float32)
    leak_low = leak_low * off_diagonal * (1.0 - down_share)[None]
    leak_up = 0.2 * jax.random.truncated_normal(jax.random.fold_in(key, 24), -3.0, 3.0, (FIELDS,) + multiway_dimension_sizes, jnp.float32)
    leak_up = leak_up * off_diagonal * down_share[None]
    return (diagonal, mixing, rate_low, rate_up, left_rate, right_rate, leak_low, leak_up)


def interface_linking_matrix(diagonal, mixing, rate, leak):
    identity_map = jnp.eye(FIELDS, dtype=jnp.float32)[:, :, None, None, None]
    inverse_part = identity_map / diagonal[:, None] - mixing / (diagonal[:, None] * diagonal[None]) + leak / diagonal[:, None]
    return -inverse_part * rate[None]


def draw_dinv(key, part):
    diagonal, mixing, rate_low, rate_up, left_rate, right_rate, leak_low, leak_up = cell_law(key)
    identity_map = jnp.eye(FIELDS, dtype=jnp.float32)[:, :, None, None, None]
    return (identity_map * diagonal[:, None] + mixing).astype(jnp.float32)


def draw_lower(key, part):
    diagonal, mixing, rate_low, rate_up, left_rate, right_rate, leak_low, leak_up = cell_law(key)
    return interface_linking_matrix(diagonal, mixing, rate_low, leak_low).astype(jnp.float32)


def draw_upper(key, part):
    diagonal, mixing, rate_low, rate_up, left_rate, right_rate, leak_low, leak_up = cell_law(key)
    return interface_linking_matrix(diagonal, mixing, rate_up, leak_up).astype(jnp.float32)


def draw_az_left(key, part):
    diagonal, mixing, rate_low, rate_up, left_rate, right_rate, leak_low, leak_up = cell_law(key)
    return (left_rate / diagonal).astype(jnp.float32)


def draw_az_right(key, part):
    diagonal, mixing, rate_low, rate_up, left_rate, right_rate, leak_low, leak_up = cell_law(key)
    return (right_rate / diagonal).astype(jnp.float32)


def draw_rhs(key, part):
    multiway_dimension_sizes = (FIELDS, TUBE_SLICES, AZALL, RAD)
    values = 0.05 * jax.random.normal(jax.random.fold_in(key, 42), multiway_dimension_sizes, jnp.float32)
    return values.astype(jnp.float32)


def draw_counts(key, part):
    drawn = jax.random.randint(jax.random.fold_in(key, 31), (SEGS, SECTORS, SECTORS), CAP // 4, CAP + 1)
    full_dest = jax.random.randint(jax.random.fold_in(key, 32), (SEGS, 1, 1), 0, SECTORS)
    dest_ids = jnp.arange(SECTORS)[None, None, :]
    return jnp.where(dest_ids == full_dest, CAP, drawn).astype(jnp.int32)


def plant(values, own_key, least, high):
    place = [jax.random.randint(jax.random.fold_in(own_key, axis), (), 0, length) for axis, length in enumerate(values.shape)]
    widest = values.shape.index(max(values.shape))
    beside = place[:widest] + [(place[widest] + 1) % values.shape[widest]] + place[widest + 1:]
    return values.at[tuple(place)].set(least).at[tuple(beside)].set(high)


def shard_levels(rng, dims, shards, low, top_value):
    level, own = 1.0, jax.random.fold_in(rng, 6)
    for dim, parts in shards:
        heights = jnp.exp(jax.random.uniform(jax.random.fold_in(own, dim), (parts,), jnp.float32, low / len(shards), top_value / len(shards)))
        level = level * jnp.repeat(heights, dims[dim] // parts).reshape([-1 if axis == dim else 1 for axis in range(len(dims))])
    return level


def gaussian(own_key, dims, deviation, limit, shards=(), kind=jnp.bfloat16):
    values = deviation * jax.random.normal(own_key, dims, jnp.float32)
    if shards:
        values = values * shard_levels(own_key, dims, shards, -0.22, 0.18)
    return jnp.clip(values, -limit, limit).astype(kind)


def setup_inputs(seed: int = 0) -> dict:
    arg_keys = jax.random.split(jax.random.key(seed), 12)
    return {
        "start_field": gaussian(arg_keys[0], (FIELDS, TUBE_SLICES, AZALL, RAD), 1.0, 6.0, ((1, 8), (2, 4)), jnp.float32),
        "rhs": draw_rhs(jax.random.fold_in(arg_keys[11], 71), 0),
        "dinv": draw_dinv(jax.random.fold_in(arg_keys[11], 71), 0),
        "lower": draw_lower(jax.random.fold_in(arg_keys[11], 71), 0),
        "upper": draw_upper(jax.random.fold_in(arg_keys[11], 71), 0),
        "az_left": draw_az_left(jax.random.fold_in(arg_keys[11], 71), 0),
        "az_right": draw_az_right(jax.random.fold_in(arg_keys[11], 71), 0),
        "counts": draw_counts(jax.random.fold_in(arg_keys[11], 71), 0),
        "receiver_cells": plant(jax.random.randint(arg_keys[8], (SEGS, SECTORS, SECTORS, CAP), 0, PLANES * AZ * RAD), jax.random.fold_in(arg_keys[8], 1), 0, (PLANES * AZ * RAD) - 1).astype(jnp.int32),
        "donor_cell": plant(jax.random.randint(arg_keys[9], (SEGS, SECTORS, SECTORS, CAP), 0, PLANES * AZ * RAD), jax.random.fold_in(arg_keys[9], 1), 0, (PLANES * AZ * RAD) - 1).astype(jnp.int32),
        "iface_weight": gaussian(arg_keys[10], (SEGS, SECTORS, FIELDS, SECTORS, CAP), 0.04, 0.25, ((0, 8), (1, 4)), jnp.float32),
    }


def apply_block(matrix, vector):
    return jnp.sum(matrix * vector[None], axis=1)


def compose(left_mat, trailing_operator):
    return jnp.sum(left_mat[:, :, None] * trailing_operator[None], axis=1)


def cycle_term(field_now, az_left, az_right):
    return az_left * jnp.roll(field_now, 1, axis=2) + az_right * jnp.roll(field_now, -1, axis=2)


def sliding_boundary_contribution(field_now, counts, receiver_cells, donor_cell, iface_weight):
    cell_count = PLANES * AZ * RAD
    blocks = field_now.reshape(FIELDS, SEGS, PLANES, SECTORS, AZ, RAD)
    blocks = jnp.transpose(blocks, (1, 3, 0, 2, 4, 5)).reshape(SEGS, SECTORS, FIELDS, cell_count)
    slot_ids = jnp.arange(CAP, dtype=jnp.int32)
    occupied = slot_ids[None, None, None, :] < counts[..., None]

    def per_segment(packed):
        block_rows, receivers, feeding_elements, weights, live_slots = packed
        picked = jax.vmap(lambda one_block, rows: one_block[:, rows])(block_rows, receivers)
        values = jnp.where(live_slots[:, None], weights * picked, 0.0)
        values = jnp.transpose(values, (2, 1, 0, 3))

        def per_dest(dest_values, dest_rows):
            empty = jnp.zeros((FIELDS, cell_count), jnp.float32)
            return empty.at[:, dest_rows.reshape(-1)].add(dest_values.reshape(FIELDS, -1))

        return jax.vmap(per_dest)(values, feeding_elements)

    result = lax.map(per_segment, (blocks, receiver_cells, donor_cell, iface_weight, occupied))
    result = result.reshape(SEGS, SECTORS, FIELDS, PLANES, AZ, RAD)
    return jnp.transpose(result, (2, 0, 3, 1, 4, 5)).reshape(FIELDS, TUBE_SLICES, AZALL, RAD)


def line_sweep(forcing_vector, dinv, coupling, reverse):
    def step_plane(previous, plane_id):
        inverse = dinv[:, :, plane_id]
        matrix = -compose(inverse, coupling[:, :, plane_id])
        driven = apply_block(inverse, forcing_vector[:, plane_id])
        updated = apply_block(matrix, previous) + driven
        return updated, updated

    start = jnp.zeros((FIELDS, AZALL, RAD), jnp.float32)
    ignored, planes_out = lax.scan(step_plane, start, jnp.arange(TUBE_SLICES, dtype=jnp.int32), reverse=reverse)
    return jnp.moveaxis(planes_out, 0, 1)


def reference(start_field, rhs, dinv, lower, upper, az_left, az_right, counts, receiver_cells, donor_cell, iface_weight):
    field_now = start_field
    for sweep_id in range(SWEEPS):
        next_planes = jnp.concatenate([field_now[:, 1:], jnp.zeros_like(field_now[:, :1])], axis=1)
        forcing_vector = rhs + cycle_term(field_now, az_left, az_right) + sliding_boundary_contribution(field_now, counts, receiver_cells, donor_cell, iface_weight) - apply_block(upper, next_planes)
        field_now = line_sweep(forcing_vector, dinv, lower, False)
        behind = jnp.concatenate([jnp.zeros_like(field_now[:, :1]), field_now[:, :-1]], axis=1)
        forcing_vector = rhs + cycle_term(field_now, az_left, az_right) + sliding_boundary_contribution(field_now, counts, receiver_cells, donor_cell, iface_weight) - apply_block(lower, behind)
        field_now = line_sweep(forcing_vector, dinv, upper, True)
    return field_now
```

```python
import functools

import jax
import jax.numpy as jnp
from jax import lax
from jax.experimental import pallas as pl
from jax.experimental.pallas import tpu as pltpu
from jax.sharding import PartitionSpec as P

SWEEPS = 2
MESH = pl.DeviceIdType.MESH
BF = jnp.bfloat16
F32 = jnp.float32


def split(x):
    hi = x.astype(BF)
    return hi, (x - hi.astype(F32)).astype(BF)


def kernel(n_ax, n_sec, start, rhs, dinv, lower, upper, azl, azr, counts, recv_cells, donor, weight, out,
           fld, low_step, high_step, maps, map_in, offs, off_in, entry, edge, halo_out, halo_in,
           slot_out, slot_in, part, drive, pick_row, pick_lane, put_row, put_lane, live_w, iface,
           map_ss, map_rs, off_ss, off_rs, edge_ss, edge_rs, halo_ss, halo_rs, slot_ss, slot_rs):
    fields, planes, az, rad = rhs.shape
    cap = recv_cells.shape[-1]
    rows = planes * az
    fr = range(fields)
    a, s = lax.axis_index("axial"), lax.axis_index("sector")
    right, left = lax.rem(s + 1, n_sec), lax.rem(s + n_sec - 1, n_sec)
    halves = 2 * SWEEPS

    barrier = pltpu.get_barrier_semaphore()
    for e in range(1, n_sec):
        pl.semaphore_signal(barrier, inc=1, device_id={"sector": lax.rem(s + e, n_sec)}, device_id_type=MESH)
    for d in range(1, n_ax):
        pl.semaphore_signal(barrier, inc=1, device_id={"axial": lax.rem(a + d, n_ax)}, device_id_type=MESH)

    def place(direction):
        return (a, 1) if direction == 0 else (n_ax - 1 - a, -1)

    def remote(src, dst, ss, rs, **device):
        return pltpu.make_async_remote_copy(src_ref=src, dst_ref=dst, send_sem=ss, recv_sem=rs,
                                            device_id=device, device_id_type=MESH)

    def peer(direction, d):
        return lax.rem(a + place(direction)[1] * d + n_ax, n_ax)

    def map_copy(direction, d):
        return remote(maps.at[direction], map_in.at[direction, d], map_ss.at[direction, d],
                      map_rs.at[direction, d], axial=peer(direction, d))

    def off_copy(h, d):
        return remote(offs.at[h], off_in.at[h, d], off_ss.at[h, d], off_rs.at[h, d], axial=peer(h % 2, d))

    def map_range(direction):
        q, _ = place(direction)
        return 1, jnp.where(q >= 1, n_ax - q, 1)

    def edge_copy():
        return remote(start.at[:, 0], edge, edge_ss.at[0], edge_rs.at[0], axial=lax.rem(a + n_ax - 1, n_ax))

    def halo_copy(h, side):
        return remote(halo_out.at[h, side], halo_in.at[h, side], halo_ss.at[h, side], halo_rs.at[h, side],
                      sector=right if side == 0 else left)

    def slot_copy(h, e, sending):
        target = lax.rem(s + e, n_sec)
        owner = s if sending else lax.rem(s + n_sec - e, n_sec)
        return remote(slot_out.at[h, target], slot_in.at[h, owner], slot_ss.at[h, e], slot_rs.at[h, e],
                      sector=target)

    def each(low, high, body):
        def step(d, c):
            body(d)
            return c
        lax.fori_loop(low, high, step, 0)

    def one_hots(cells, row_ref, lane_ref):
        down = lax.broadcasted_iota(jnp.int32, (rows, cap), 0)
        across = lax.broadcasted_iota(jnp.int32, (rad, cap), 0)
        for t in range(n_sec):
            idx = cells[0, 0, pl.ds(t, 1), :]
            cols = slice(t * cap, (t + 1) * cap)
            row_ref[0:rows, cols] = jnp.where(down == idx // rad, 1.0, 0.0).astype(BF)
            lane_ref[:, cols] = jnp.where(across == lax.rem(idx, rad), 1.0, 0.0)

    def times(mat, p, x):
        return [sum(mat[i, j, p] * x[j] for j in fr) for i in fr]

    def send_field(h):
        for side, layer in ((0, az - 1), (1, 0)):
            halo_out[h, side] = fld[:, 1:planes + 1, layer, :]
        for side in range(2):
            halo_copy(h, side).start()
        for f in fr:
            turned = fld[f, 1:planes + 1].reshape(rows, rad).T
            hi, lo = split(turned)
            got = (jnp.dot(hi, pick_row[...], preferred_element_type=F32)
                   + jnp.dot(lo, pick_row[...], preferred_element_type=F32))
            line = jnp.sum(got * pick_lane[...], axis=0, keepdims=True) * live_w[pl.ds(f, 1), :]
            for t in range(n_sec):
                slot_out[h, t, pl.ds(f, 1), :] = line[:, t * cap:(t + 1) * cap]
        for e in range(1, n_sec):
            slot_copy(h, e, True).start()
        slot_in[h, s] = slot_out[h, s]

    def build_map(coupling, steps, direction):
        for i in fr:
            for j in fr:
                maps[direction, i, j] = jnp.full((az, rad), 1.0 if i == j else 0.0, F32)

        def step(i, c):
            p = i if direction == 0 else planes - 1 - i
            for col in fr:
                v = times(dinv, p, [coupling[j, col, p] for j in fr])
                for r in fr:
                    steps[r, col, p] = -v[r]
            for col in fr:
                v = times(steps, p, [maps[direction, j, col] for j in fr])
                for r in fr:
                    maps[direction, r, col] = v[r]
            return c

        lax.fori_loop(0, planes, step, 0)
        each(*map_range(direction), lambda d: map_copy(direction, d).start())

    row_id = lax.broadcasted_iota(jnp.int32, (az, rad), 0)

    def half(h):
        direction = h % 2
        coupling, steps = (upper, low_step) if direction == 0 else (lower, high_step)
        ahead = 2 if direction == 0 else 0
        q, _ = place(direction)

        def local_part(p, c):
            other = times(coupling, p, [fld[j, p + ahead] for j in fr])
            for f in fr:
                v = fld[f, p + 1]
                before = jnp.where(row_id == 0, 0.0, pltpu.roll(v, 1, 0))
                after = jnp.where(row_id == az - 1, 0.0, pltpu.roll(v, az - 1, 0))
                part[f, p] = rhs[f, p] + azl[f, p] * before + azr[f, p] * after - other[f]
            return c

        lax.fori_loop(0, planes, local_part, 0)

        for e in range(1, n_sec):
            slot_copy(h, e, False).wait_recv()
        for f in fr:
            line = jnp.concatenate([slot_in[h, t, pl.ds(f, 1), :] for t in range(n_sec)], axis=1)
            hi, lo = split(put_lane[...] * line)
            dims = (((1,), (1,)), ((), ()))
            iface[f] = (lax.dot_general(put_row[...], hi, dims, preferred_element_type=F32)
                        + lax.dot_general(put_row[...], lo, dims, preferred_element_type=F32))
        for side in range(2):
            halo_copy(h, side).wait_recv()

        def forward(i, y):
            p = i if direction == 0 else planes - 1 - i
            source = []
            for f in fr:
                before = jnp.where(row_id == 0, halo_in[h, 0, f, pl.ds(p, 1), :], 0.0)
                after = jnp.where(row_id == az - 1, halo_in[h, 1, f, pl.ds(p, 1), :], 0.0)
                source.append(part[f, p] + azl[f, p] * before + azr[f, p] * after
                              + iface[f, pl.ds(pl.multiple_of(p * az, az), az), :])
            driven = times(dinv, p, source)
            for f in fr:
                drive[f, p] = driven[f]
            moved = times(steps, p, y)
            return tuple(moved[f] + driven[f] for f in fr)

        zero = tuple(jnp.zeros((az, rad), F32) for _ in fr)
        y = lax.fori_loop(0, planes, forward, zero)
        for f in fr:
            offs[h, f] = y[f]
        each(1, n_ax - q, lambda d: off_copy(h, d).start())
        if h == 0:
            build_map(upper, high_step, 1)
        if h < 2:
            each(1, q, lambda d: map_copy(direction, d).wait_recv())

        entry[...] = jnp.zeros_like(entry)

        @pl.when(q > 0)
        def _():
            off_copy(h, q).wait_recv()
            entry[...] = off_in[h, q]

            def absorb(i, c):
                d = q - i
                off_copy(h, d).wait_recv()
                x = [entry[j] for j in fr]
                for r in fr:
                    entry[r] = sum(map_in[direction, d, r, j] * x[j] for j in fr) + off_in[h, d, r]
                return c

            lax.fori_loop(1, q, absorb, 0)

        for f in fr:
            fld[f, 0 if direction == 0 else planes + 1] = entry[f]

        def replay(i, x):
            p = i if direction == 0 else planes - 1 - i
            moved = times(steps, p, x)
            new = tuple(moved[f] + drive[f, p] for f in fr)
            for f in fr:
                if h == halves - 1:
                    out[f, p] = new[f]
                else:
                    fld[f, p + 1] = new[f]
            return new

        lax.fori_loop(0, planes, replay, tuple(entry[f] for f in fr))

    fld[:, 1:planes + 1] = start[...]
    one_hots(recv_cells, pick_row, pick_lane)
    slot_id = lax.broadcasted_iota(jnp.int32, (1, cap), 1)
    for t in range(n_sec):
        for f in fr:
            live_w[pl.ds(f, 1), t * cap:(t + 1) * cap] = jnp.where(
                slot_id < counts[0, 0, t], weight[0, 0, f, pl.ds(t, 1), :], 0.0)
    for t in range(n_sec):
        for h in range(halves):
            slot_out[h, t] = jnp.zeros_like(slot_out[h, t])
    pl.semaphore_wait(barrier, n_sec - 1 + n_ax - 1)

    @pl.when(a > 0)
    def _():
        edge_copy().start()

    send_field(0)
    build_map(lower, low_step, 0)
    one_hots(donor, put_row, put_lane)

    @pl.when(a < n_ax - 1)
    def _():
        edge_copy().wait_recv()
        fld[:, planes + 1] = edge[...]

    @pl.when(a == n_ax - 1)
    def _():
        fld[:, planes + 1] = jnp.zeros_like(edge)

    for h in range(halves):
        if h:
            send_field(h)
        half(h)

    @pl.when(a > 0)
    def _():
        edge_copy().wait_send()

    for direction in range(2):
        each(*map_range(direction), lambda d: map_copy(direction, d).wait_send())
    for h in range(halves):
        q, _ = place(h % 2)
        each(1, n_ax - q, lambda d: off_copy(h, d).wait_send())
        for side in range(2):
            halo_copy(h, side).wait_send()
        for e in range(1, n_sec):
            slot_copy(h, e, True).wait_send()


def shards(n_ax, n_sec, *args):
    fields, planes, az, rad = args[0].shape
    cap = args[8].shape[-1]
    rows, slots, halves = planes * az, n_sec * cap, 2 * SWEEPS
    vm, dma = pltpu.VMEM, pltpu.SemaphoreType.DMA
    square, line = (fields, fields), (az, rad)
    vmem = pl.BlockSpec(memory_space=pltpu.VMEM)
    specs = [vmem] * 7 + [pl.BlockSpec(memory_space=pltpu.SMEM)] + [vmem] * 3
    return pl.pallas_call(
        functools.partial(kernel, n_ax, n_sec),
        out_shape=jax.ShapeDtypeStruct(args[0].shape, F32),
        in_specs=specs,
        out_specs=vmem,
        scratch_shapes=[
            vm((fields, planes + 2) + line, F32),
            vm(square + (planes,) + line, F32),
            vm(square + (planes,) + line, F32),
            vm((2,) + square + line, F32),
            vm((2, n_ax) + square + line, F32),
            vm((halves, fields) + line, F32),
            vm((halves, n_ax, fields) + line, F32),
            vm((fields,) + line, F32),
            vm((fields,) + line, F32),
            vm((halves, 2, fields, planes, rad), F32),
            vm((halves, 2, fields, planes, rad), F32),
            vm((halves, n_sec, 8, cap), F32),
            vm((halves, n_sec, 8, cap), F32),
            vm((fields, planes) + line, F32),
            vm((fields, planes) + line, F32),
            vm((rows, slots), BF),
            vm((rad, slots), F32),
            vm((rows, slots), BF),
            vm((rad, slots), F32),
            vm((8, slots), F32),
            vm((fields, rows, rad), F32),
            dma((2, n_ax)), dma((2, n_ax)),
            dma((halves, n_ax)), dma((halves, n_ax)),
            dma((1,)), dma((1,)),
            dma((halves, 2)), dma((halves, 2)),
            dma((halves, n_sec)), dma((halves, n_sec)),
        ],
        compiler_params=pltpu.CompilerParams(
            collective_id=0, has_side_effects=True, vmem_limit_bytes=48 * 1024 * 1024
        ),
    )(*args)


def solution(mesh):
    in_specs = (
        P(None, "axial", "sector", None),
        P(None, "axial", "sector", None),
        P(None, None, "axial", "sector", None),
        P(None, None, "axial", "sector", None),
        P(None, None, "axial", "sector", None),
        P(None, "axial", "sector", None),
        P(None, "axial", "sector", None),
        P("axial", "sector", None),
        P("axial", "sector", None, None),
        P("axial", "sector", None, None),
        P("axial", "sector", None, None, None),
    )
    body = functools.partial(shards, mesh.shape["axial"], mesh.shape["sector"])
    return jax.shard_map(body, mesh=mesh, in_specs=in_specs,
                         out_specs=P(None, "axial", "sector", None), check_vma=False)
```

```python
import functools

import jax
import jax.numpy as jnp
from jax import lax
from jax.experimental import pallas as pl
from jax.experimental.pallas import tpu as pltpu
from jax.sharding import PartitionSpec as P

SWEEPS = 2
MESH = pl.DeviceIdType.MESH
BF = jnp.bfloat16
F32 = jnp.float32


def split(x):
    hi = x.astype(BF)
    return hi, (x - hi.astype(F32)).astype(BF)


def dot5(left, right):
    terms = [x * y for x, y in zip(left, right)]
    while len(terms) > 1:
        terms = [sum(terms[i + 1:i + 2], terms[i]) for i in range(0, len(terms), 2)]
    return terms[0]


def kernel(n_ax, n_sec, *refs):
    (start_h, rhs_h, dinv_h, lower_h, upper_h, azl_h, azr_h, counts, cells_h, donor_h, weight_h, out,
     start, rhs, dinv, lower, upper, azl, azr, recv_cells, donor, weight, in_sem, fld, low_step, high_step, maps, mate_map, late_map, pair_map, map_in, offs, mate_off, pair_off, off_in, entry,
     edge, halo_out, halo_in, slot_out, slot_in, part, drive, pick_row, pick_lane, put_row, put_lane, live_w, iface,
     mate_ss, mate_rs, map_ss, map_rs, off_ss, off_rs, edge_ss, edge_rs, halo_ss, halo_rs, slot_ss, slot_rs) = refs
    fields, planes, az, rad = rhs.shape
    cap = recv_cells.shape[-1]
    rows = planes * az
    fr = range(fields)
    a, s = lax.axis_index("axial"), lax.axis_index("sector")
    right, left = lax.rem(s + 1, n_sec), lax.rem(s + n_sec - 1, n_sec)
    halves = 2 * SWEEPS

    loads = [pltpu.make_async_copy(src, dst, in_sem.at[i]) for i, (src, dst) in enumerate([
        (start_h, start), (cells_h, recv_cells), (weight_h, weight), (dinv_h, dinv), (lower_h, lower),
        (upper_h, upper), (rhs_h, rhs), (azl_h, azl), (azr_h, azr), (donor_h, donor)])]
    for load in loads:
        load.start()

    barrier = pltpu.get_barrier_semaphore()
    for e in range(1, n_sec):
        pl.semaphore_signal(barrier, inc=1, device_id={"sector": lax.rem(s + e, n_sec)}, device_id_type=MESH)
    for d in range(1, n_ax):
        pl.semaphore_signal(barrier, inc=1, device_id={"axial": lax.rem(a + d, n_ax)}, device_id_type=MESH)

    n_pair = n_ax // 2

    def place(direction):
        q = a if direction == 0 else n_ax - 1 - a
        return q // 2, lax.rem(q, 2)

    def remote(src, dst, ss, rs, **device):
        return pltpu.make_async_remote_copy(src_ref=src, dst_ref=dst, send_sem=ss, recv_sem=rs,
                                            device_id=device, device_id_type=MESH)

    mate = a + 1 - 2 * lax.rem(a, 2)

    def peer(direction, d):
        return lax.rem(a + (2 * d if direction == 0 else 2 * (n_ax - d)), n_ax)

    def mate_copy(src, dst, k):
        return remote(src, dst, mate_ss.at[k], mate_rs.at[k], axial=mate)

    def mate_map_copy(direction):
        return mate_copy(maps.at[direction], mate_map.at[direction], 2 * SWEEPS + direction)

    def mate_off_copy(h):
        return mate_copy(offs.at[h], mate_off.at[h], h)

    def map_copy(direction, d):
        return remote(pair_map.at[direction], map_in.at[direction, d], map_ss.at[direction, d],
                      map_rs.at[direction, d], axial=peer(direction, d))

    def off_copy(h, d):
        return remote(pair_off.at[h], off_in.at[h, d], off_ss.at[h, d], off_rs.at[h, d], axial=peer(h % 2, d))

    def map_range(direction):
        z, _ = place(direction)
        return 1, jnp.where(z >= 1, n_pair - z, 1)

    def edge_copy():
        return remote(start.at[:, 0], edge, edge_ss.at[0], edge_rs.at[0], axial=lax.rem(a + n_ax - 1, n_ax))

    def halo_copy(h, side):
        return remote(halo_out.at[h, side], halo_in.at[h, side], halo_ss.at[h, side], halo_rs.at[h, side],
                      sector=right if side == 0 else left)

    def slot_copy(h, e, sending):
        target = lax.rem(s + e, n_sec)
        owner = s if sending else lax.rem(s + n_sec - e, n_sec)
        return remote(slot_out.at[h, target], slot_in.at[h, owner], slot_ss.at[h, e], slot_rs.at[h, e],
                      sector=target)

    def each(low, high, body):
        def step(d, c):
            body(d)
            return c
        lax.fori_loop(low, high, step, 0)

    def one_hots(cells, row_ref, lane_ref):
        down = lax.broadcasted_iota(jnp.int32, (rows, cap), 0)
        across = lax.broadcasted_iota(jnp.int32, (rad, cap), 0)
        for t in range(n_sec):
            idx = cells[0, 0, pl.ds(t, 1), :]
            cols = slice(t * cap, (t + 1) * cap)
            row_ref[0:rows, cols] = jnp.where(down == idx // rad, 1.0, 0.0).astype(BF)
            lane_ref[:, cols] = jnp.where(across == lax.rem(idx, rad), 1.0, 0.0)

    def times(mat, p, x):
        return [dot5([mat[i, j, p] for j in fr], x) for i in fr]

    def send_field(h):
        for side, layer in ((0, az - 1), (1, 0)):
            halo_out[h, side] = fld[:, 1:planes + 1, layer, :]
        for side in range(2):
            halo_copy(h, side).start()
        for f in fr:
            turned = fld[f, 1:planes + 1].reshape(rows, rad).T
            hi, lo = split(turned)
            got = (jnp.dot(hi, pick_row[...], preferred_element_type=F32)
                   + jnp.dot(lo, pick_row[...], preferred_element_type=F32))
            line = jnp.sum(got * pick_lane[...], axis=0, keepdims=True) * live_w[pl.ds(f, 1), :]
            for t in range(n_sec):
                slot_out[h, t, pl.ds(f, 1), :] = line[:, t * cap:(t + 1) * cap]
        for e in range(1, n_sec):
            slot_copy(h, e, True).start()
        slot_in[h, s] = slot_out[h, s]

    def build_map(coupling, steps, direction):
        for i in fr:
            for j in fr:
                maps[direction, i, j] = jnp.full((az, rad), 1.0 if i == j else 0.0, F32)

        def step(i, c):
            p = i if direction == 0 else planes - 1 - i
            for col in fr:
                v = times(dinv, p, [coupling[j, col, p] for j in fr])
                for r in fr:
                    steps[r, col, p] = -v[r]
            for col in fr:
                v = times(steps, p, [maps[direction, j, col] for j in fr])
                for r in fr:
                    maps[direction, r, col] = v[r]
            return c

        lax.fori_loop(0, planes, step, 0, unroll=4)
        mate_map_copy(direction).start()

    def pair_up(direction):
        _, late = place(direction)
        mate_map_copy(direction).wait_recv()
        for r in fr:
            for j in fr:
                late_map[direction, r, j] = jnp.where(late == 1, maps[direction, r, j], mate_map[direction, r, j])
        for col in fr:
            first = [jnp.where(late == 1, mate_map[direction, j, col], maps[direction, j, col]) for j in fr]
            for r in fr:
                pair_map[direction, r, col] = dot5([late_map[direction, r, j] for j in fr], first)
        each(*map_range(direction), lambda d: map_copy(direction, d).start())

    row_id = lax.broadcasted_iota(jnp.int32, (az, rad), 0)

    def half(h):
        direction = h % 2
        coupling, steps = (upper, low_step) if direction == 0 else (lower, high_step)
        ahead = 2 if direction == 0 else 0
        z, late = place(direction)

        def local_part(p, c):
            other = times(coupling, p, [fld[j, p + ahead] for j in fr])
            for f in fr:
                v = fld[f, p + 1]
                before = jnp.where(row_id == 0, 0.0, pltpu.roll(v, 1, 0))
                after = jnp.where(row_id == az - 1, 0.0, pltpu.roll(v, az - 1, 0))
                part[f, p] = rhs[f, p] + azl[f, p] * before + azr[f, p] * after - other[f]
            return c

        lax.fori_loop(0, planes, local_part, 0, unroll=16)
        if h == 1:
            pair_up(1)

        for e in range(1, n_sec):
            slot_copy(h, e, False).wait_recv()
        for f in fr:
            line = jnp.concatenate([slot_in[h, t, pl.ds(f, 1), :] for t in range(n_sec)], axis=1)
            hi, lo = split(put_lane[...] * line)
            dims = (((1,), (1,)), ((), ()))
            iface[f] = (lax.dot_general(put_row[...], hi, dims, preferred_element_type=F32)
                        + lax.dot_general(put_row[...], lo, dims, preferred_element_type=F32))
        for side in range(2):
            halo_copy(h, side).wait_recv()

        def forward(i, y):
            p = i if direction == 0 else planes - 1 - i
            source = []
            for f in fr:
                before = jnp.where(row_id == 0, halo_in[h, 0, f, pl.ds(p, 1), :], 0.0)
                after = jnp.where(row_id == az - 1, halo_in[h, 1, f, pl.ds(p, 1), :], 0.0)
                source.append(part[f, p] + azl[f, p] * before + azr[f, p] * after
                              + iface[f, pl.ds(pl.multiple_of(p * az, az), az), :])
            driven = times(dinv, p, source)
            for f in fr:
                drive[f, p] = driven[f]
            moved = times(steps, p, y)
            return tuple(moved[f] + driven[f] for f in fr)

        zero = tuple(jnp.zeros((az, rad), F32) for _ in fr)
        y = lax.fori_loop(0, planes, forward, zero, unroll=16)
        for f in fr:
            offs[h, f] = y[f]
        mate_off_copy(h).start()
        if h == 0:
            pair_up(0)
        mate_off_copy(h).wait_recv()
        first = [jnp.where(late == 1, mate_off[h, j], y[j]) for j in fr]
        for r in fr:
            last = jnp.where(late == 1, y[r], mate_off[h, r])
            pair_off[h, r] = dot5([late_map[direction, r, j] for j in fr], first) + last
        each(1, n_pair - z, lambda d: off_copy(h, d).start())
        if h == 0:
            build_map(upper, high_step, 1)
        if h < 2:
            each(1, z, lambda d: map_copy(direction, d).wait_recv())

        entry[...] = jnp.zeros_like(entry)

        @pl.when(z > 0)
        def _():
            off_copy(h, z).wait_recv()
            entry[...] = off_in[h, z]

            def absorb(i, c):
                d = z - i
                off_copy(h, d).wait_recv()
                x = [entry[j] for j in fr]
                for r in fr:
                    entry[r] = dot5([map_in[direction, d, r, j] for j in fr], x) + off_in[h, d, r]
                return c

            lax.fori_loop(1, z, absorb, 0)

        @pl.when(late == 1)
        def _():
            x = [entry[j] for j in fr]
            for r in fr:
                entry[r] = dot5([mate_map[direction, r, j] for j in fr], x) + mate_off[h, r]

        for f in fr:
            fld[f, 0 if direction == 0 else planes + 1] = entry[f]

        def replay(i, x):
            p = i if direction == 0 else planes - 1 - i
            moved = times(steps, p, x)
            new = tuple(moved[f] + drive[f, p] for f in fr)
            for f in fr:
                if h == halves - 1:
                    out[f, p] = new[f]
                else:
                    fld[f, p + 1] = new[f]
            return new

        lax.fori_loop(0, planes, replay, tuple(entry[f] for f in fr), unroll=16)

    for load in loads[:3]:
        load.wait()
    fld[:, 1:planes + 1] = start[...]
    one_hots(recv_cells, pick_row, pick_lane)
    slot_id = lax.broadcasted_iota(jnp.int32, (1, cap), 1)
    for t in range(n_sec):
        for f in fr:
            live_w[pl.ds(f, 1), t * cap:(t + 1) * cap] = jnp.where(
                slot_id < counts[0, 0, t], weight[0, 0, f, pl.ds(t, 1), :], 0.0)
    for t in range(n_sec):
        for h in range(halves):
            slot_out[h, t] = jnp.zeros_like(slot_out[h, t])
    pl.semaphore_wait(barrier, n_sec - 1 + n_ax - 1)

    @pl.when(a > 0)
    def _():
        edge_copy().start()

    send_field(0)
    for load in loads[3:]:
        load.wait()
    build_map(lower, low_step, 0)
    one_hots(donor, put_row, put_lane)

    @pl.when(a < n_ax - 1)
    def _():
        edge_copy().wait_recv()
        fld[:, planes + 1] = edge[...]

    @pl.when(a == n_ax - 1)
    def _():
        fld[:, planes + 1] = jnp.zeros_like(edge)

    for h in range(halves):
        if h:
            send_field(h)
        half(h)

    @pl.when(a > 0)
    def _():
        edge_copy().wait_send()

    for direction in range(2):
        mate_map_copy(direction).wait_send()
        each(*map_range(direction), lambda d: map_copy(direction, d).wait_send())
    for h in range(halves):
        z, _ = place(h % 2)
        mate_off_copy(h).wait_send()
        each(1, n_pair - z, lambda d: off_copy(h, d).wait_send())
        for side in range(2):
            halo_copy(h, side).wait_send()
        for e in range(1, n_sec):
            slot_copy(h, e, True).wait_send()


def shards(n_ax, n_sec, *args):
    fields, planes, az, rad = args[0].shape
    cap = args[8].shape[-1]
    rows, slots, halves = planes * az, n_sec * cap, 2 * SWEEPS
    vm, dma = pltpu.VMEM, pltpu.SemaphoreType.DMA
    square, line = (fields, fields), (az, rad)
    vmem = pl.BlockSpec(memory_space=pltpu.VMEM)
    hbm = pl.BlockSpec(memory_space=pltpu.HBM)
    specs = [hbm] * 7 + [pl.BlockSpec(memory_space=pltpu.SMEM)] + [hbm] * 3
    return pl.pallas_call(
        functools.partial(kernel, n_ax, n_sec),
        out_shape=jax.ShapeDtypeStruct(args[0].shape, F32),
        in_specs=specs,
        out_specs=vmem,
        scratch_shapes=[vm(x.shape, x.dtype) for x in args[:7] + args[8:]] + [
            dma((10,)),
            vm((fields, planes + 2) + line, F32),
            vm(square + (planes,) + line, F32),
            vm(square + (planes,) + line, F32),
            vm((2,) + square + line, F32),
            vm((2,) + square + line, F32),
            vm((2,) + square + line, F32),
            vm((2,) + square + line, F32),
            vm((2, n_ax // 2) + square + line, F32),
            vm((halves, fields) + line, F32),
            vm((halves, fields) + line, F32),
            vm((halves, fields) + line, F32),
            vm((halves, n_ax // 2, fields) + line, F32),
            vm((fields,) + line, F32),
            vm((fields,) + line, F32),
            vm((halves, 2, fields, planes, rad), F32),
            vm((halves, 2, fields, planes, rad), F32),
            vm((halves, n_sec, 8, cap), F32),
            vm((halves, n_sec, 8, cap), F32),
            vm((fields, planes) + line, F32),
            vm((fields, planes) + line, F32),
            vm((rows, slots), BF),
            vm((rad, slots), F32),
            vm((rows, slots), BF),
            vm((rad, slots), F32),
            vm((8, slots), F32),
            vm((fields, rows, rad), F32),
            dma((halves + 2,)), dma((halves + 2,)),
            dma((2, n_ax // 2)), dma((2, n_ax // 2)),
            dma((halves, n_ax // 2)), dma((halves, n_ax // 2)),
            dma((1,)), dma((1,)),
            dma((halves, 2)), dma((halves, 2)),
            dma((halves, n_sec)), dma((halves, n_sec)),
        ],
        compiler_params=pltpu.CompilerParams(
            collective_id=0, has_side_effects=True, vmem_limit_bytes=48 * 1024 * 1024
        ),
    )(*args)


def solution(mesh):
    in_specs = (
        P(None, "axial", "sector", None),
        P(None, "axial", "sector", None),
        P(None, None, "axial", "sector", None),
        P(None, None, "axial", "sector", None),
        P(None, None, "axial", "sector", None),
        P(None, "axial", "sector", None),
        P(None, "axial", "sector", None),
        P("axial", "sector", None),
        P("axial", "sector", None, None),
        P("axial", "sector", None, None),
        P("axial", "sector", None, None, None),
    )
    body = functools.partial(shards, mesh.shape["axial"], mesh.shape["sector"])
    return jax.shard_map(body, mesh=mesh, in_specs=in_specs,
                         out_specs=P(None, "axial", "sector", None), check_vma=False)
```

```python
import functools

import jax
import jax.numpy as jnp
from jax import lax
from jax.experimental import pallas as pl
from jax.experimental.pallas import tpu as pltpu
from jax.sharding import PartitionSpec as P

SWEEPS = 2
MESH = pl.DeviceIdType.MESH
BF = jnp.bfloat16
F32 = jnp.float32


def split(x):
    hi = x.astype(BF)
    return hi, (x - hi.astype(F32)).astype(BF)


def dot5(left, right):
    terms = [x * y for x, y in zip(left, right)]
    while len(terms) > 1:
        terms = [sum(terms[i + 1:i + 2], terms[i]) for i in range(0, len(terms), 2)]
    return terms[0]


def kernel(n_ax, n_sec, *refs):
    (start_h, rhs_h, dinv_h, lower_h, upper_h, azl_h, azr_h, counts, cells_h, donor_h, weight_h, out,
     start, rhs, dinv, lower, upper, azl, azr, recv_cells, donor, weight, in_sem, fld, low_step, high_step, maps, mate_map, late_map, pair_map, map_in, offs, mate_off, pair_off, off_in, entry,
     edge, halo_out, halo_in, slot_out, slot_in, part, drive, pick_row, pick_lane, put_row, put_lane, live_w, iface,
     mate_ss, mate_rs, map_ss, map_rs, off_ss, off_rs, edge_ss, edge_rs, halo_ss, halo_rs, slot_ss, slot_rs) = refs
    fields, planes, az, rad = rhs.shape
    cap = recv_cells.shape[-1]
    rows = planes * az
    fr = range(fields)
    a, s = lax.axis_index("axial"), lax.axis_index("sector")
    right, left = lax.rem(s + 1, n_sec), lax.rem(s + n_sec - 1, n_sec)
    halves = 2 * SWEEPS

    loads = [pltpu.make_async_copy(src, dst, in_sem.at[i]) for i, (src, dst) in enumerate([
        (start_h, start), (cells_h, recv_cells), (weight_h, weight), (dinv_h, dinv), (lower_h, lower),
        (upper_h, upper), (rhs_h, rhs), (azl_h, azl), (azr_h, azr), (donor_h, donor)])]
    for load in loads:
        load.start()

    barrier = pltpu.get_barrier_semaphore()
    for e in range(1, n_sec):
        pl.semaphore_signal(barrier, inc=1, device_id={"sector": lax.rem(s + e, n_sec)}, device_id_type=MESH)
    for d in range(1, n_ax):
        pl.semaphore_signal(barrier, inc=1, device_id={"axial": lax.rem(a + d, n_ax)}, device_id_type=MESH)

    n_pair = n_ax // 2

    def place(direction):
        q = a if direction == 0 else n_ax - 1 - a
        return q // 2, lax.rem(q, 2)

    def remote(src, dst, ss, rs, **device):
        return pltpu.make_async_remote_copy(src_ref=src, dst_ref=dst, send_sem=ss, recv_sem=rs,
                                            device_id=device, device_id_type=MESH)

    mate = a + 1 - 2 * lax.rem(a, 2)

    def peer(direction, d):
        return lax.rem(a + (2 * d if direction == 0 else 2 * (n_ax - d)), n_ax)

    def mate_copy(src, dst, k):
        return remote(src, dst, mate_ss.at[k], mate_rs.at[k], axial=mate)

    def mate_map_copy(direction):
        return mate_copy(maps.at[direction], mate_map.at[direction], 2 * SWEEPS + direction)

    def mate_off_copy(h):
        return mate_copy(offs.at[h], mate_off.at[h], h)

    def map_copy(direction, d):
        return remote(pair_map.at[direction], map_in.at[direction, d], map_ss.at[direction, d],
                      map_rs.at[direction, d], axial=peer(direction, d))

    def off_copy(h, d):
        return remote(pair_off.at[h], off_in.at[h, d], off_ss.at[h, d], off_rs.at[h, d], axial=peer(h % 2, d))

    def map_range(direction):
        z, _ = place(direction)
        return 1, jnp.where(z >= 1, n_pair - z, 1)

    def edge_copy():
        return remote(start.at[:, 0], edge, edge_ss.at[0], edge_rs.at[0], axial=lax.rem(a + n_ax - 1, n_ax))

    def halo_copy(h, side):
        return remote(halo_out.at[h, side], halo_in.at[h, side], halo_ss.at[h, side], halo_rs.at[h, side],
                      sector=right if side == 0 else left)

    def slot_copy(h, e, sending):
        target = lax.rem(s + e, n_sec)
        owner = s if sending else lax.rem(s + n_sec - e, n_sec)
        return remote(slot_out.at[h, target], slot_in.at[h, owner], slot_ss.at[h, e], slot_rs.at[h, e],
                      sector=target)

    def each(low, high, body):
        def step(d, c):
            body(d)
            return c
        lax.fori_loop(low, high, step, 0)

    def one_hots(cells, row_ref, lane_ref):
        down = lax.broadcasted_iota(jnp.int32, (rows, cap), 0)
        across = lax.broadcasted_iota(jnp.int32, (rad, cap), 0)
        for t in range(n_sec):
            idx = cells[0, 0, pl.ds(t, 1), :]
            cols = slice(t * cap, (t + 1) * cap)
            row_ref[0:rows, cols] = jnp.where(down == idx // rad, 1.0, 0.0).astype(BF)
            lane_ref[:, cols] = jnp.where(across == lax.rem(idx, rad), 1.0, 0.0)

    def times(mat, p, x):
        return [dot5([mat[i, j, p] for j in fr], x) for i in fr]

    def send_field(h):
        for side, layer in ((0, az - 1), (1, 0)):
            halo_out[h, side] = fld[:, 1:planes + 1, layer, :]
        for side in range(2):
            halo_copy(h, side).start()
        for f in fr:
            turned = fld[f, 1:planes + 1].reshape(rows, rad).T
            hi, lo = split(turned)
            got = (jnp.dot(hi, pick_row[...], preferred_element_type=F32)
                   + jnp.dot(lo, pick_row[...], preferred_element_type=F32))
            line = jnp.sum(got * pick_lane[...], axis=0, keepdims=True) * live_w[pl.ds(f, 1), :]
            for t in range(n_sec):
                slot_out[h, t, pl.ds(f, 1), :] = line[:, t * cap:(t + 1) * cap]
        for e in range(1, n_sec):
            slot_copy(h, e, True).start()
        slot_in[h, s] = slot_out[h, s]

    def build_map(coupling, steps, direction):
        for i in fr:
            for j in fr:
                maps[direction, i, j] = jnp.full((az, rad), 1.0 if i == j else 0.0, F32)

        def step(i, c):
            p = i if direction == 0 else planes - 1 - i
            for col in fr:
                v = times(dinv, p, [coupling[j, col, p] for j in fr])
                for r in fr:
                    steps[r, col, p] = -v[r]
            for col in fr:
                v = times(steps, p, [maps[direction, j, col] for j in fr])
                for r in fr:
                    maps[direction, r, col] = v[r]
            return c

        lax.fori_loop(0, planes, step, 0, unroll=4)

    def pair_up(direction):
        _, late = place(direction)
        mate_map_copy(direction).wait_recv()
        for r in fr:
            for j in fr:
                late_map[direction, r, j] = jnp.where(late == 1, maps[direction, r, j], mate_map[direction, r, j])
        for col in fr:
            first = [jnp.where(late == 1, mate_map[direction, j, col], maps[direction, j, col]) for j in fr]
            for r in fr:
                pair_map[direction, r, col] = dot5([late_map[direction, r, j] for j in fr], first)
        each(*map_range(direction), lambda d: map_copy(direction, d).start())

    row_id = lax.broadcasted_iota(jnp.int32, (az, rad), 0)

    def half(h):
        direction = h % 2
        coupling, steps = (upper, low_step) if direction == 0 else (lower, high_step)
        ahead = 2 if direction == 0 else 0
        z, late = place(direction)

        def local_part(p, c):
            other = times(coupling, p, [fld[j, p + ahead] for j in fr])
            for f in fr:
                v = fld[f, p + 1]
                before = jnp.where(row_id == 0, 0.0, pltpu.roll(v, 1, 0))
                after = jnp.where(row_id == az - 1, 0.0, pltpu.roll(v, az - 1, 0))
                part[f, p] = rhs[f, p] + azl[f, p] * before + azr[f, p] * after - other[f]
            return c

        lax.fori_loop(0, planes, local_part, 0, unroll=16)
        if h == 1:
            pair_up(1)

        for e in range(1, n_sec):
            slot_copy(h, e, False).wait_recv()
        for f in fr:
            line = jnp.concatenate([slot_in[h, t, pl.ds(f, 1), :] for t in range(n_sec)], axis=1)
            hi, lo = split(put_lane[...] * line)
            dims = (((1,), (1,)), ((), ()))
            iface[f] = (lax.dot_general(put_row[...], hi, dims, preferred_element_type=F32)
                        + lax.dot_general(put_row[...], lo, dims, preferred_element_type=F32))
        for side in range(2):
            halo_copy(h, side).wait_recv()

        def forward(i, y):
            p = i if direction == 0 else planes - 1 - i
            source = []
            for f in fr:
                before = jnp.where(row_id == 0, halo_in[h, 0, f, pl.ds(p, 1), :], 0.0)
                after = jnp.where(row_id == az - 1, halo_in[h, 1, f, pl.ds(p, 1), :], 0.0)
                source.append(part[f, p] + azl[f, p] * before + azr[f, p] * after
                              + iface[f, pl.ds(pl.multiple_of(p * az, az), az), :])
            driven = times(dinv, p, source)
            for f in fr:
                drive[f, p] = driven[f]
            moved = times(steps, p, y)
            return tuple(moved[f] + driven[f] for f in fr)

        zero = tuple(jnp.zeros((az, rad), F32) for _ in fr)
        y = lax.fori_loop(0, planes, forward, zero, unroll=16)
        for f in fr:
            offs[h, f] = y[f]
        mate_off_copy(h).start()
        if h == 0:
            pair_up(0)
        mate_off_copy(h).wait_recv()
        first = [jnp.where(late == 1, mate_off[h, j], y[j]) for j in fr]
        for r in fr:
            last = jnp.where(late == 1, y[r], mate_off[h, r])
            pair_off[h, r] = dot5([late_map[direction, r, j] for j in fr], first) + last
        each(1, n_pair - z, lambda d: off_copy(h, d).start())
        if h < 2:
            each(1, z, lambda d: map_copy(direction, d).wait_recv())

        entry[...] = jnp.zeros_like(entry)

        @pl.when(z > 0)
        def _():
            off_copy(h, z).wait_recv()
            entry[...] = off_in[h, z]

            def absorb(i, c):
                d = z - i
                off_copy(h, d).wait_recv()
                x = [entry[j] for j in fr]
                for r in fr:
                    entry[r] = dot5([map_in[direction, d, r, j] for j in fr], x) + off_in[h, d, r]
                return c

            lax.fori_loop(1, z, absorb, 0)

        @pl.when(late == 1)
        def _():
            x = [entry[j] for j in fr]
            for r in fr:
                entry[r] = dot5([mate_map[direction, r, j] for j in fr], x) + mate_off[h, r]

        for f in fr:
            fld[f, 0 if direction == 0 else planes + 1] = entry[f]

        def replay(i, x):
            p = i if direction == 0 else planes - 1 - i
            moved = times(steps, p, x)
            new = tuple(moved[f] + drive[f, p] for f in fr)
            for f in fr:
                if h == halves - 1:
                    out[f, p] = new[f]
                else:
                    fld[f, p + 1] = new[f]
            return new

        lax.fori_loop(0, planes, replay, tuple(entry[f] for f in fr), unroll=16)

    for load in loads[:3]:
        load.wait()
    fld[:, 1:planes + 1] = start[...]
    one_hots(recv_cells, pick_row, pick_lane)
    slot_id = lax.broadcasted_iota(jnp.int32, (1, cap), 1)
    for t in range(n_sec):
        for f in fr:
            live_w[pl.ds(f, 1), t * cap:(t + 1) * cap] = jnp.where(
                slot_id < counts[0, 0, t], weight[0, 0, f, pl.ds(t, 1), :], 0.0)
    for t in range(n_sec):
        for h in range(halves):
            slot_out[h, t] = jnp.zeros_like(slot_out[h, t])
    for load in loads[3:]:
        load.wait()
    build_map(lower, low_step, 0)
    pl.semaphore_wait(barrier, n_sec - 1 + n_ax - 1)

    @pl.when(a > 0)
    def _():
        edge_copy().start()

    mate_map_copy(0).start()
    send_field(0)
    build_map(upper, high_step, 1)
    mate_map_copy(1).start()
    one_hots(donor, put_row, put_lane)

    @pl.when(a < n_ax - 1)
    def _():
        edge_copy().wait_recv()
        fld[:, planes + 1] = edge[...]

    @pl.when(a == n_ax - 1)
    def _():
        fld[:, planes + 1] = jnp.zeros_like(edge)

    for h in range(halves):
        if h:
            send_field(h)
        half(h)

    @pl.when(a > 0)
    def _():
        edge_copy().wait_send()

    for direction in range(2):
        mate_map_copy(direction).wait_send()
        each(*map_range(direction), lambda d: map_copy(direction, d).wait_send())
    for h in range(halves):
        z, _ = place(h % 2)
        mate_off_copy(h).wait_send()
        each(1, n_pair - z, lambda d: off_copy(h, d).wait_send())
        for side in range(2):
            halo_copy(h, side).wait_send()
        for e in range(1, n_sec):
            slot_copy(h, e, True).wait_send()


def shards(n_ax, n_sec, *args):
    fields, planes, az, rad = args[0].shape
    cap = args[8].shape[-1]
    rows, slots, halves = planes * az, n_sec * cap, 2 * SWEEPS
    vm, dma = pltpu.VMEM, pltpu.SemaphoreType.DMA
    square, line = (fields, fields), (az, rad)
    vmem = pl.BlockSpec(memory_space=pltpu.VMEM)
    hbm = pl.BlockSpec(memory_space=pltpu.HBM)
    specs = [hbm] * 7 + [pl.BlockSpec(memory_space=pltpu.SMEM)] + [hbm] * 3
    return pl.pallas_call(
        functools.partial(kernel, n_ax, n_sec),
        out_shape=jax.ShapeDtypeStruct(args[0].shape, F32),
        in_specs=specs,
        out_specs=vmem,
        scratch_shapes=[vm(x.shape, x.dtype) for x in args[:7] + args[8:]] + [
            dma((10,)),
            vm((fields, planes + 2) + line, F32),
            vm(square + (planes,) + line, F32),
            vm(square + (planes,) + line, F32),
            vm((2,) + square + line, F32),
            vm((2,) + square + line, F32),
            vm((2,) + square + line, F32),
            vm((2,) + square + line, F32),
            vm((2, n_ax // 2) + square + line, F32),
            vm((halves, fields) + line, F32),
            vm((halves, fields) + line, F32),
            vm((halves, fields) + line, F32),
            vm((halves, n_ax // 2, fields) + line, F32),
            vm((fields,) + line, F32),
            vm((fields,) + line, F32),
            vm((halves, 2, fields, planes, rad), F32),
            vm((halves, 2, fields, planes, rad), F32),
            vm((halves, n_sec, 8, cap), F32),
            vm((halves, n_sec, 8, cap), F32),
            vm((fields, planes) + line, F32),
            vm((fields, planes) + line, F32),
            vm((rows, slots), BF),
            vm((rad, slots), F32),
            vm((rows, slots), BF),
            vm((rad, slots), F32),
            vm((8, slots), F32),
            vm((fields, rows, rad), F32),
            dma((halves + 2,)), dma((halves + 2,)),
            dma((2, n_ax // 2)), dma((2, n_ax // 2)),
            dma((halves, n_ax // 2)), dma((halves, n_ax // 2)),
            dma((1,)), dma((1,)),
            dma((halves, 2)), dma((halves, 2)),
            dma((halves, n_sec)), dma((halves, n_sec)),
        ],
        compiler_params=pltpu.CompilerParams(
            collective_id=0, has_side_effects=True, vmem_limit_bytes=48 * 1024 * 1024
        ),
    )(*args)


def solution(mesh):
    in_specs = (
        P(None, "axial", "sector", None),
        P(None, "axial", "sector", None),
        P(None, None, "axial", "sector", None),
        P(None, None, "axial", "sector", None),
        P(None, None, "axial", "sector", None),
        P(None, "axial", "sector", None),
        P(None, "axial", "sector", None),
        P("axial", "sector", None),
        P("axial", "sector", None, None),
        P("axial", "sector", None, None),
        P("axial", "sector", None, None, None),
    )
    body = functools.partial(shards, mesh.shape["axial"], mesh.shape["sector"])
    return jax.shard_map(body, mesh=mesh, in_specs=in_specs,
                         out_specs=P(None, "axial", "sector", None), check_vma=False)
```
